512 devices in a mesh: stn: 32 (over x, y_lo, core), tm: 16 (over y_hi, z).
Axes of the slice: x: 4, y: 8 (y_hi: 2, y_lo: 4; y = y_hi * 4 + y_lo), z: 8, core: 2. Of those that a mesh axis runs over, the one named last changes fastest.
Arguments:
- samples: bfloat16 [512, 2, 491520], P('stn', None, 'tm'), may hold values from -6 to 6
- filter_taps: float32 [16, 384], replicated, may hold values from -1.5 to 1.5
- frac_delay: float32 [512], P('stn'), may hold values from 0 to 1
- station_delay: int32 [512], P('stn'), may hold values from 0 to 1536, as said below
- beam_index: int32 [500, 512], replicated, may hold values from 0 to 255
Outputs:
- beam_power: float32 [384, 500, 1280], P('stn', None, 'tm')
The draws below stay inside these ranges and needn't reach their ends.
Inputs may be any that keep to these rules, and one draw needn't show every extreme that they name: `station_delay`: every station's delay lies in 0 to 1536; some station has exactly 1536.
All inputs are finite; a program needn't handle non-finite values.
Results may differ from the reference program's by a relative error of at most 0.0053.
Values may be sent and summed in bfloat16 or wider, within the bound.
A program may use at most 128 MiB of HBM per device.

```python
import math
import jax
import jax.numpy as jnp
from jax import lax

S = 512
C = 384
B = 500
P_SIZE = 16
DSPEC = 4
TIME = 491520


def draw_station_delay(key, part):
    first_key, second_key = jax.random.split(jax.random.fold_in(key, 7))
    drawn_delays = jax.random.randint(first_key, (S,), 0, DSPEC * C + 1, dtype=jnp.int32)
    chosen = jax.random.randint(second_key, (), 0, S, dtype=jnp.int32)
    positions = jnp.arange(S, dtype=jnp.int32)
    return jnp.where(positions == chosen, DSPEC * C, drawn_delays).astype(jnp.int32)


def set_ends(drawn, key, low, largest):
    longest = drawn.shape.index(max(drawn.shape))
    spots = []
    for shift in (0, 1):
        where = [jax.random.randint(jax.random.fold_in(key, axis), (), 0, length) for axis, length in enumerate(drawn.shape)]
        where[longest] = (where[longest] + shift) % drawn.shape[longest]
        spots.append(tuple(where))
    return drawn.at[spots[0]].set(low).at[spots[1]].set(largest)


def block_levels(key, dims, cuts, low, high):
    factor_of, own = 1.0, jax.random.fold_in(key, 6)
    for dim, parts in cuts:
        steps = jnp.exp(jax.random.uniform(jax.random.fold_in(own, dim), (parts,), jnp.float32, low / len(cuts), high / len(cuts)))
        factor_of = factor_of * jnp.repeat(steps, dims[dim] // parts).reshape([-1 if axis == dim else 1 for axis in range(len(dims))])
    return factor_of


def scatter_about(stream_key, dims, scale, limit, shards=(), kind=jnp.bfloat16):
    gain = block_levels(stream_key, dims, shards, -0.22, 0.18) if shards else 1.0
    array = jax.random.normal(stream_key, dims, jnp.float32) * scale * gain
    return jnp.minimum(jnp.maximum(array, -limit), limit).astype(kind)


def setup_inputs(seed: int = 0) -> dict:
    streams_of = jax.random.split(jax.random.key(seed), 6)
    samples = scatter_about(streams_of[0], (S, 2, TIME), 1.0, 6.0, ((0, 32), (2, 16)))
    filter_taps = scatter_about(streams_of[1], (P_SIZE, C), P_SIZE ** -0.5, 1.5, (), jnp.float32)
    frac_delay = jnp.clip(1.0 * jax.random.uniform(streams_of[2], (S,), jnp.float32) ** block_levels(streams_of[2], (S,), ((0, 32),), -0.2, 0.2), 0.0, 1.0)
    station_delay = draw_station_delay(jax.random.fold_in(streams_of[5], 71), 0)
    beam_index = set_ends(jax.random.randint(streams_of[4], (B, S), 0, 256), jax.random.fold_in(streams_of[4], 1), 0, 255).astype(jnp.int32)
    return dict(samples=samples, filter_taps=filter_taps, frac_delay=frac_delay, station_delay=station_delay, beam_index=beam_index)


def dft_table(width):
    counter = jnp.arange(width, dtype=jnp.int32)
    product = counter[:, None] * counter[None, :] % width
    angle = 2.0 * math.pi / width * product.astype(jnp.float32)
    factor = 1.0 / math.sqrt(width)
    cosine = jnp.cos(angle) * factor
    sine = jnp.sin(angle) * factor
    upper = jnp.concatenate([cosine, -sine], axis=1)
    lower = jnp.concatenate([sine, cosine], axis=1)
    return jnp.concatenate([upper, lower], axis=0).astype(jnp.bfloat16)

def polyphase(delayed, filter_taps, table, frac_delay):
    stations = delayed.shape[0]
    taps, width = filter_taps.shape
    spectra = delayed.shape[2] // width - taps + 1
    blocks = delayed.reshape(stations, 2, spectra + taps - 1, width)
    summed = jnp.zeros((stations, 2, spectra, width), jnp.float32)
    for tap_index in range(taps):
        summed = summed + blocks[:, :, tap_index:tap_index + spectra, :].astype(jnp.float32) * filter_taps[tap_index]
    frames = summed.astype(jnp.bfloat16).transpose(0, 2, 1, 3).reshape(stations * spectra, 2 * width)
    spectrum = jnp.dot(frames, table, preferred_element_type=jnp.float32).reshape(stations, spectra, 2, width)
    offsets = (jnp.arange(width, dtype=jnp.int32) - width // 2).astype(jnp.float32)
    phase = 2.0 * math.pi / width * frac_delay[:, None] * offsets[None, :]
    cosine = jnp.cos(phase)[:, None, :]
    sine = jnp.sin(phase)[:, None, :]
    real_part = spectrum[:, :, 0, :]
    imag_part = spectrum[:, :, 1, :]
    rotated_re = real_part * cosine - imag_part * sine
    rotated_im = real_part * sine + imag_part * cosine
    return jnp.stack([rotated_re, rotated_im], axis=1).astype(jnp.bfloat16)

def detect_beams(beam_index, channel, data, width, spectra):
    product = beam_index * (channel - width // 2) % (16 * width)
    angle = 2.0 * math.pi / (16 * width) * product.astype(jnp.float32)
    weight_re = jnp.cos(angle).astype(jnp.bfloat16)
    weight_im = jnp.sin(angle).astype(jnp.bfloat16)
    first = jnp.dot(weight_re, data, preferred_element_type=jnp.float32)
    second = jnp.dot(weight_im, data, preferred_element_type=jnp.float32)
    beam_re = first[:, :spectra] - second[:, spectra:]
    beam_im = first[:, spectra:] + second[:, :spectra]
    return (beam_re * beam_re + beam_im * beam_im) / beam_index.shape[1]

def reference(samples, filter_taps, frac_delay, station_delay, beam_index):
    width = C
    taps = P_SIZE
    spectra = samples.shape[2] // width
    padded = jnp.pad(samples, ((0, 0), (0, 0), (0, (taps - 1 + DSPEC) * width)))
    table = dft_table(width)
    length = (spectra + taps - 1) * width

    def one_station(packed):
        station_row, delay_value, frac_value = packed
        delayed = lax.dynamic_slice_in_dim(station_row, delay_value, length, 1)
        return polyphase(delayed[None], filter_taps, table, frac_value[None])[0]
    phased = lax.map(one_station, (padded, station_delay, frac_delay))
    by_channel = phased.transpose(3, 0, 1, 2).reshape(width, phased.shape[0], 2 * spectra)

    def one_channel(packed):
        channel, data = packed
        return detect_beams(beam_index, channel, data, width, spectra)
    return lax.map(one_channel, (jnp.arange(width, dtype=jnp.int32), by_channel))
```

```python
import functools
import math

import jax
import jax.numpy as jnp
import ml_dtypes
import numpy as np
from jax import lax
from jax.experimental import pallas as pl
from jax.experimental.pallas import tpu as pltpu
from jax.sharding import PartitionSpec as P

TAPS = 16
C = 384
B = 500
LANES = 128
COLS = C // LANES
DSPEC = 4
STN = 32
ST = 16
KS = 80
KG = KS // 16
GROUPS = 3
CPG = 4
REACH = (TAPS - 1 + DSPEC) * C
SPAN = KS * C
DCOLS = (KS + TAPS - 1) * COLS
MESH = pl.DeviceIdType.MESH


def sincos_turns(r):
    h = r * math.pi
    z = h * h
    s = jnp.full_like(r, 1.0 / 6227020800.0)
    for c in (-1.0 / 39916800.0, 1.0 / 362880.0, -1.0 / 5040.0, 1.0 / 120.0, -1.0 / 6.0, 1.0):
        s = s * z + c
    s = s * h
    q = jnp.full_like(r, 1.0 / 479001600.0)
    for c in (-1.0 / 3628800.0, 1.0 / 40320.0, -1.0 / 720.0, 1.0 / 24.0, -0.5, 1.0):
        q = q * z + c
    return 1.0 - 2.0 * s * s, 2.0 * s * q


def column_channels():
    lane = np.arange(LANES)
    dest, sub = lane % STN, lane // STN
    own = C // STN
    return np.stack([dest * own + g * CPG + sub for g in range(GROUPS)])


def dft_columns():
    chan = column_channels()
    n = np.arange(C)
    parts = []
    for g in range(GROUPS):
        angle = 2.0 * np.pi / C * ((n[:, None] * chan[g][None, :]) % C)
        cosine = np.cos(angle) / math.sqrt(C)
        sine = np.sin(angle) / math.sqrt(C)
        upper = np.concatenate([cosine, -sine], axis=1)
        lower = np.concatenate([sine, cosine], axis=1)
        parts.append(np.concatenate([upper, lower], axis=0))
    return np.stack(parts).astype(ml_dtypes.bfloat16)


def polyphase_kernel(main_ref, halo_ref, delay_ref, taps_ref, f_ref, ext, dly):
    delay = jnp.broadcast_to(delay_ref[...], (ST, LANES))
    lane = lax.broadcasted_iota(jnp.int32, (ST, LANES), 1)
    rest = delay & (LANES - 1)
    index = (lane + rest) & (LANES - 1)
    keep = lane < LANES - rest
    bits = [(delay & (LANES << b)) != 0 for b in range(4)]
    total = (SPAN + REACH) // LANES
    for r in range(2):
        ext[r, :, :SPAN] = main_ref[r].astype(jnp.float32)
        ext[r, :, SPAN:] = halo_ref[r].astype(jnp.float32)

    chunk = 15

    def align(step, _):
        base = step * chunk
        for r in range(2):
            cols = []
            for j in range(chunk + 16):
                at = pl.multiple_of(jnp.minimum(base + j, total - 1) * LANES, LANES)
                cols.append(ext[r, :, pl.ds(at, LANES)])
            for b in (3, 2, 1, 0):
                cols = [jnp.where(bits[b], cols[j + (1 << b)], cols[j]) for j in range(len(cols) - (1 << b))]
            turned = [
                jnp.take_along_axis(col, index, axis=1, mode="promise_in_bounds")
                for col in cols[: chunk + 1]
            ]
            for j in range(chunk):
                at = pl.multiple_of((base + j) * LANES, LANES)
                dly[r, :, pl.ds(at, LANES)] = jnp.where(keep, turned[j], turned[j + 1])
        return 0

    lax.fori_loop(0, DCOLS // chunk, align, 0)

    per = 8

    def filt(step, _):
        for r in range(2):
            for m in range(COLS):
                sums = [None] * per
                for j in range(per + TAPS - 1):
                    at = pl.multiple_of((step * per + j) * C + m * LANES, LANES)
                    col = dly[r, :, pl.ds(at, LANES)]
                    for i in range(max(0, j - TAPS + 1), min(per, j + 1)):
                        p = j - i
                        term = col * taps_ref[p : p + 1, m * LANES : (m + 1) * LANES]
                        sums[i] = term if sums[i] is None else sums[i] + term
                for i in range(per):
                    row = pl.multiple_of((step * per + i) * ST, ST)
                    f_ref[pl.ds(row, ST), r * C + m * LANES : r * C + (m + 1) * LANES] = sums[i].astype(jnp.bfloat16)
        return 0

    lax.fori_loop(0, KS // per, filt, 0)


def polyphase(main, halo, delay, taps):
    vmem = pl.BlockSpec(memory_space=pltpu.VMEM)
    return pl.pallas_call(
        polyphase_kernel,
        out_shape=jax.ShapeDtypeStruct((KS * ST, 2 * C), jnp.bfloat16),
        in_specs=[vmem] * 4,
        out_specs=vmem,
        scratch_shapes=[
            pltpu.VMEM((2, ST, SPAN + REACH), jnp.float32),
            pltpu.VMEM((2, ST, DCOLS * LANES), jnp.float32),
        ],
        compiler_params=pltpu.CompilerParams(vmem_limit_bytes=40 << 20),
    )(main, halo, delay, taps)


def butterfly(vregs, lane, widths):
    vregs = list(vregs)
    for j, w in enumerate(widths):
        mask = (lane & w) != 0
        out = list(vregs)
        for i in range(len(vregs)):
            if not i & (1 << j):
                k = i | (1 << j)
                out[i] = jnp.where(mask, pltpu.roll(vregs[k], w, 1), vregs[i])
                out[k] = jnp.where(mask, vregs[k], pltpu.roll(vregs[i], LANES - w, 1))
        vregs = out
    return vregs


def beam_kernel(f_ref, table_ref, offset_ref, frac_ref, index_ref, out_ref, msg, recv, weights, rhs, send_sem, recv_sem, own_sem):
    me = lax.axis_index("stn")
    barrier = pltpu.get_barrier_semaphore()

    def greet(i, _):
        pl.semaphore_signal(barrier, inc=1, device_id={"stn": lax.rem(me + i, STN)}, device_id_type=MESH)
        return 0

    lax.fori_loop(1, STN, greet, 0)
    lane = lax.broadcasted_iota(jnp.int32, (ST, LANES), 1)

    for g in range(GROUPS):
        phase = frac_ref[...] * offset_ref[g : g + 1, :]
        cosine, sine = sincos_turns(phase)

        def spectra(kg, _):
            rows = pl.ds(pl.multiple_of(kg * 256, 256), 256)
            spec = jnp.dot(f_ref[rows, :], table_ref[g], preferred_element_type=jnp.float32)
            turned = [[], []]
            for k in range(16):
                re = spec[k * ST : (k + 1) * ST, :LANES]
                im = spec[k * ST : (k + 1) * ST, LANES:]
                turned[0].append((re * cosine - im * sine).astype(jnp.bfloat16))
                turned[1].append((re * sine + im * cosine).astype(jnp.bfloat16))
            blocks = butterfly(turned[0] + turned[1], lane, (1, 2, 4, 8, 16))
            for d in range(STN):
                msg[g, d, kg] = blocks[d]
            return 0

        lax.fori_loop(0, KG, spectra, 0)
        if g == 0:
            pl.semaphore_wait(barrier, STN - 1)

        def post(i, _):
            to = lax.rem(me + i, STN)
            pltpu.make_async_remote_copy(
                src_ref=msg.at[g, to],
                dst_ref=recv.at[g, me],
                send_sem=send_sem.at[g],
                recv_sem=recv_sem.at[g],
                device_id={"stn": to},
                device_id_type=MESH,
            ).start()
            return 0

        lax.fori_loop(1, STN, post, 0)
        pltpu.make_async_copy(msg.at[g, me], recv.at[g, me], own_sem.at[g]).start()

    own = C // STN
    first = (me * own - C // 2).astype(jnp.float32)

    def weigh(at, rows):
        index = index_ref[pl.ds(at, rows), :].astype(jnp.float32)
        step = index * (1.0 / (16 * C))
        start = index * first * (1.0 / (16 * C))
        step_re, step_im = sincos_turns(step)
        now_re, now_im = sincos_turns(start - jnp.round(start))
        for c in range(own):
            weights[c, pl.ds(at, rows), :512] = now_re.astype(jnp.bfloat16)
            weights[c, pl.ds(at, rows), 512:] = now_im.astype(jnp.bfloat16)
            if c < own - 1:
                now_re, now_im = now_re * step_re - now_im * step_im, now_re * step_im + now_im * step_re

    def weigh_step(i, _):
        weigh(pl.multiple_of(i * 16, 16), 16)
        return 0

    lax.fori_loop(0, 512 // 16, weigh_step, 0)

    zero = jnp.zeros((ST, LANES), jnp.bfloat16)
    for g in range(GROUPS):
        pltpu.make_async_copy(msg.at[g, 0 : STN - 1], recv.at[g, 0 : STN - 1], recv_sem.at[g]).wait()
        pltpu.make_async_copy(msg.at[g, me], recv.at[g, me], own_sem.at[g]).wait()

        def unpack(e, _):
            blocks = [recv[g, e, kg] for kg in range(KG)] + [zero] * (8 - KG)
            blocks = butterfly(blocks, lane, (16, 32, 64))
            upper = pl.ds(pl.multiple_of(e * ST, ST), ST)
            lower = pl.ds(pl.multiple_of(512 + e * ST, ST), ST)
            for c in range(CPG):
                re, im = blocks[2 * c], blocks[2 * c + 1]
                rhs[c, upper, :LANES] = re
                rhs[c, upper, LANES:] = im
                rhs[c, lower, :LANES] = -im
                rhs[c, lower, LANES:] = re
            return 0

        lax.fori_loop(0, STN, unpack, 0)

        def detect(c, _):
            beam = jnp.dot(weights[g * CPG + c], rhs[c], preferred_element_type=jnp.float32)
            re = beam[:, :LANES]
            im = beam[:, LANES:]
            power = (re * re + im * im) * (1.0 / 512)
            out_ref[g * CPG + c] = power[:B, :KS]
            return 0

        lax.fori_loop(0, CPG, detect, 0)

    for g in range(GROUPS):
        pltpu.make_async_copy(msg.at[g, 0 : STN - 1], recv.at[g, 0 : STN - 1], send_sem.at[g]).wait()


def beams(f, table, offset, frac, index):
    vmem = pl.BlockSpec(memory_space=pltpu.VMEM)
    own = C // STN
    return pl.pallas_call(
        beam_kernel,
        out_shape=jax.ShapeDtypeStruct((own, B, KS), jnp.float32),
        in_specs=[vmem] * 5,
        out_specs=vmem,
        scratch_shapes=[
            pltpu.VMEM((GROUPS, STN, KG, ST, LANES), jnp.bfloat16),
            pltpu.VMEM((GROUPS, STN, KG, ST, LANES), jnp.bfloat16),
            pltpu.VMEM((own, 512, 1024), jnp.bfloat16),
            pltpu.VMEM((CPG, 1024, 2 * LANES), jnp.bfloat16),
            pltpu.SemaphoreType.DMA((GROUPS,)),
            pltpu.SemaphoreType.DMA((GROUPS,)),
            pltpu.SemaphoreType.DMA((GROUPS,)),
        ],
        compiler_params=pltpu.CompilerParams(collective_id=0, has_side_effects=True, vmem_limit_bytes=56 << 20),
    )(f, table, offset, frac, index)


def local(samples, filter_taps, frac_delay, station_delay, beam_index):
    count = lax.axis_size("tm")
    head = samples[:, :, :REACH]
    halo = lax.ppermute(head, "tm", [(i, i - 1) for i in range(1, count)])
    main = samples.transpose(1, 0, 2)
    halo = halo.transpose(1, 0, 2)
    f = polyphase(main, halo, station_delay[:, None], filter_taps)
    table = jnp.asarray(dft_columns())
    offset = jnp.asarray((column_channels() - C // 2).astype(np.float32) / C)
    index = jnp.pad(beam_index, ((0, 512 - B), (0, 0)))
    return beams(f, table, offset, frac_delay[:, None], index)


def solution(mesh):
    in_specs = (P("stn", None, "tm"), P(), P("stn"), P("stn"), P())
    out_specs = P("stn", None, "tm")
    return jax.shard_map(local, mesh=mesh, in_specs=in_specs, out_specs=out_specs, check_vma=False)
```

```python
import math

import jax
import jax.numpy as jnp
import ml_dtypes
import numpy as np
from jax import lax
from jax.experimental import pallas as pl
from jax.experimental.pallas import tpu as pltpu
from jax.sharding import PartitionSpec as P

TAPS = 16
C = 384
B = 500
LANES = 128
COLS = C // LANES
DSPEC = 4
STN = 32
ST = 16
KS = 80
KG = KS // 16
GROUPS = 3
CPG = 4
REACH = (TAPS - 1 + DSPEC) * C
SPAN = KS * C
DCOLS = (KS + TAPS - 1) * COLS
PHASES = ((0, 1), (1, 3), (3, 5))
CHUNK = 24
RIM = (TAPS - 1) * COLS + 48 * PHASES[-1][0]
RIM_COLS = SPAN // LANES - RIM
EXT_COLS = DCOLS + 16 - RIM
MESH = pl.DeviceIdType.MESH


def sincos_turns(r):
    h = r * math.pi
    z = h * h
    s = jnp.full_like(r, 1.0 / 6227020800.0)
    for c in (-1.0 / 39916800.0, 1.0 / 362880.0, -1.0 / 5040.0, 1.0 / 120.0, -1.0 / 6.0, 1.0):
        s = s * z + c
    s = s * h
    q = jnp.full_like(r, 1.0 / 479001600.0)
    for c in (-1.0 / 3628800.0, 1.0 / 40320.0, -1.0 / 720.0, 1.0 / 24.0, -0.5, 1.0):
        q = q * z + c
    return 1.0 - 2.0 * s * s, 2.0 * s * q


def column_channels():
    lane = np.arange(LANES)
    dest, sub = lane % STN, lane // STN
    own = C // STN
    return np.stack([dest * own + g * CPG + sub for g in range(GROUPS)])


def dft_columns():
    chan = column_channels()
    n = np.arange(C)
    parts = []
    for g in range(GROUPS):
        angle = 2.0 * np.pi / C * ((n[:, None] * chan[g][None, :]) % C)
        cosine = np.cos(angle) / math.sqrt(C)
        sine = np.sin(angle) / math.sqrt(C)
        upper = np.concatenate([cosine, -sine], axis=1)
        lower = np.concatenate([sine, cosine], axis=1)
        parts.append(np.concatenate([upper, lower], axis=0))
    return np.stack(parts).astype(ml_dtypes.bfloat16)


def butterfly(vregs, lane, widths):
    vregs = list(vregs)
    for j, w in enumerate(widths):
        mask = (lane & w) != 0
        out = list(vregs)
        for i in range(len(vregs)):
            if not i & (1 << j):
                k = i | (1 << j)
                out[i] = jnp.where(mask, pltpu.roll(vregs[k], w, 1), vregs[i])
                out[k] = jnp.where(mask, vregs[k], pltpu.roll(vregs[i], LANES - w, 1))
        vregs = out
    return vregs


def station_rows(values_ref):
    row = lax.broadcasted_iota(jnp.int32, (ST, LANES), 0)
    out = jnp.full((ST, LANES), values_ref[0])
    for i in range(1, ST):
        out = jnp.where(row == i, values_ref[i], out)
    return out


def kernel(main_ref, delay_ref, frac_ref, taps_ref, table_ref, offset_ref, index_ref, out_ref, ext, dly, frames, msg, recv, weights, rhs, power, send_sem, recv_sem, own_sem, halo_sem, out_sem):
    me = lax.axis_index("stn")
    tm = lax.axis_index("tm")
    count = lax.axis_size("tm")
    barrier = pltpu.get_barrier_semaphore()

    def greet(i, _):
        pl.semaphore_signal(barrier, inc=1, device_id={"stn": lax.rem(me + i, STN)}, device_id_type=MESH)
        return 0

    lax.fori_loop(1, STN, greet, 0)
    pl.semaphore_signal(barrier, inc=1, device_id={"tm": lax.rem(tm + 1, count)}, device_id_type=MESH)

    delay = station_rows(delay_ref)
    frac = station_rows(frac_ref)
    lane = lax.broadcasted_iota(jnp.int32, (ST, LANES), 1)
    rest = delay & (LANES - 1)
    index = (lane + rest) & (LANES - 1)
    keep = lane < LANES - rest
    bits = [(delay & (LANES << b)) != 0 for b in range(4)]

    ext[:, :, : RIM_COLS * LANES] = main_ref[:, :, RIM * LANES :]
    ext[:, :, RIM_COLS * LANES + REACH :] = jnp.zeros((2, ST, EXT_COLS * LANES - RIM_COLS * LANES - REACH), jnp.bfloat16)

    pl.semaphore_wait(barrier, STN)

    def halo(to):
        return pltpu.make_async_remote_copy(
            src_ref=main_ref.at[:, :, :REACH],
            dst_ref=ext.at[:, :, RIM_COLS * LANES : RIM_COLS * LANES + REACH],
            send_sem=halo_sem.at[0],
            recv_sem=halo_sem.at[1],
            device_id={"tm": to},
            device_id_type=MESH,
        )

    @pl.when(tm > 0)
    def _():
        halo(tm - 1).start()

    @pl.when(tm == count - 1)
    def _():
        ext[:, :, RIM_COLS * LANES : RIM_COLS * LANES + REACH] = jnp.zeros((2, ST, REACH), jnp.bfloat16)

    def align(source, base, shift):
        for r in range(2):
            cols = []
            for j in range(CHUNK + 16):
                at = pl.multiple_of((base + j - shift) * LANES, LANES)
                cols.append(source[r, :, pl.ds(at, LANES)])
            for b in (3, 2, 1, 0):
                cols = [jnp.where(bits[b], cols[j + (1 << b)], cols[j]) for j in range(len(cols) - (1 << b))]
            turned = [
                jnp.take_along_axis(col.astype(jnp.float32), index, axis=1, mode="promise_in_bounds")
                for col in cols[: CHUNK + 1]
            ]
            for j in range(CHUNK):
                at = pl.multiple_of((base + j) * LANES, LANES)
                dly[r, :, pl.ds(at, LANES)] = jnp.where(keep, turned[j], turned[j + 1])

    per = 8

    def filt(step):
        for r in range(2):
            for m in range(COLS):
                sums = [None] * per
                for j in range(per + TAPS - 1):
                    at = pl.multiple_of((step * per + j) * C + m * LANES, LANES)
                    col = dly[r, :, pl.ds(at, LANES)]
                    for i in range(max(0, j - TAPS + 1), min(per, j + 1)):
                        p = j - i
                        term = col * taps_ref[p : p + 1, m * LANES : (m + 1) * LANES]
                        sums[i] = term if sums[i] is None else sums[i] + term
                for i in range(per):
                    row = pl.multiple_of((step * per + i) * ST, ST)
                    frames[pl.ds(row, ST), r * C + m * LANES : r * C + (m + 1) * LANES] = sums[i].astype(jnp.bfloat16)

    def spectra(g, kg, cosine, sine):
        spec = jnp.dot(frames[kg * 256 : (kg + 1) * 256, :], table_ref[g], preferred_element_type=jnp.float32)
        turned = [[], []]
        for k in range(16):
            re = spec[k * ST : (k + 1) * ST, :LANES]
            im = spec[k * ST : (k + 1) * ST, LANES:]
            turned[0].append((re * cosine - im * sine).astype(jnp.bfloat16))
            turned[1].append((re * sine + im * cosine).astype(jnp.bfloat16))
        blocks = butterfly(turned[0] + turned[1], lane, (1, 2, 4, 8, 16))
        for d in range(STN):
            msg[g, d, kg] = blocks[d]

    def loop(start, stop, step):
        def body(i, _):
            step(i)
            return 0

        lax.fori_loop(start, stop, body, 0)

    loop(0, 48 // CHUNK, lambda i: align(main_ref, i * CHUNK, 0))
    for number, (begin, end) in enumerate(PHASES):
        last = number == len(PHASES) - 1
        if last:
            @pl.when(tm < count - 1)
            def _():
                halo(tm).wait_recv()

        source, shift = (ext, RIM) if last else (main_ref, 0)
        first_col = (TAPS - 1) * COLS + 48 * begin
        loop(0, (end - begin) * 48 // CHUNK, lambda i: align(source, first_col + i * CHUNK, shift))
        loop(begin * 16 // per, end * 16 // per, filt)
        for g in range(GROUPS):
            cosine, sine = sincos_turns(frac * offset_ref[g : g + 1, :])
            for kg in range(begin, end):
                spectra(g, kg, cosine, sine)

            def post(i, _):
                to = lax.rem(me + i, STN)
                pltpu.make_async_remote_copy(
                    src_ref=msg.at[g, to, begin:end],
                    dst_ref=recv.at[g, me, begin:end],
                    send_sem=send_sem.at[g],
                    recv_sem=recv_sem.at[g],
                    device_id={"stn": to},
                    device_id_type=MESH,
                ).start()
                return 0

            lax.fori_loop(1, STN, post, 0)
            if last:
                pltpu.make_async_copy(msg.at[g, me], recv.at[g, me], own_sem.at[g]).start()

    own = C // STN
    first = (me * own - C // 2).astype(jnp.float32)

    def weigh(at, rows):
        rows = rows.astype(jnp.float32)
        step_re, step_im = sincos_turns(rows * (1.0 / (16 * C)))
        start = rows * first * (1.0 / (16 * C))
        now_re, now_im = sincos_turns(start - jnp.round(start))
        for c in range(own):
            weights[c, pl.ds(at, 16), :512] = now_re.astype(jnp.bfloat16)
            weights[c, pl.ds(at, 16), 512:] = now_im.astype(jnp.bfloat16)
            if c < own - 1:
                now_re, now_im = now_re * step_re - now_im * step_im, now_re * step_im + now_im * step_re

    def weigh_step(i):
        at = pl.multiple_of(i * 16, 16)
        weigh(at, index_ref[pl.ds(at, 16), :])

    loop(0, B // 16, weigh_step)
    tail = B // 16 * 16
    weigh(tail, jnp.concatenate([index_ref[tail:, :], jnp.zeros((16 - B % 16, 512), jnp.int32)], axis=0))

    per_step = 4
    wide = lax.broadcasted_iota(jnp.int32, (per_step * ST, LANES), 1)
    zero = jnp.zeros((per_step * ST, LANES), jnp.bfloat16)
    for g in range(GROUPS):
        pltpu.make_async_copy(msg.at[g, 0 : STN - 1], recv.at[g, 0 : STN - 1], recv_sem.at[g]).wait()
        pltpu.make_async_copy(msg.at[g, me], recv.at[g, me], own_sem.at[g]).wait()

        def unpack(e):
            blocks = [recv[g, pl.ds(e * per_step, per_step), kg].reshape(per_step * ST, LANES) for kg in range(KG)]
            blocks = butterfly(blocks + [zero] * (8 - KG), wide, (16, 32, 64))
            upper = pl.ds(pl.multiple_of(e * per_step * ST, per_step * ST), per_step * ST)
            lower = pl.ds(pl.multiple_of(512 + e * per_step * ST, per_step * ST), per_step * ST)
            for c in range(CPG):
                re, im = blocks[2 * c], blocks[2 * c + 1]
                rhs[c, upper, :LANES] = re
                rhs[c, upper, LANES:] = im
                rhs[c, lower, :LANES] = -im
                rhs[c, lower, LANES:] = re

        loop(0, STN // per_step, unpack)

        def detect(c):
            beam = jnp.dot(weights[g * CPG + c], rhs[c], preferred_element_type=jnp.float32)
            re = beam[:, :LANES]
            im = beam[:, LANES:]
            square = (re * re + im * im) * (1.0 / 512)
            power[g * CPG + c] = square[:B, :KS]
            pltpu.make_async_copy(power.at[g * CPG + c], out_ref.at[g * CPG + c], out_sem).start()

        loop(0, CPG, detect)

    for g in range(GROUPS):
        pltpu.make_async_copy(msg.at[g, 0 : STN - 1], recv.at[g, 0 : STN - 1], send_sem.at[g]).wait()

    @pl.when(tm > 0)
    def _():
        halo(tm).wait_send()

    pltpu.make_async_copy(power, out_ref, out_sem).wait()


def beams(main, delay, frac, taps, table, offset, index):
    vmem = pl.BlockSpec(memory_space=pltpu.VMEM)
    smem = pl.BlockSpec(memory_space=pltpu.SMEM)
    own = C // STN
    return pl.pallas_call(
        kernel,
        out_shape=jax.ShapeDtypeStruct((own, B, KS), jnp.float32),
        in_specs=[vmem, smem, smem, vmem, vmem, vmem, vmem],
        out_specs=pl.BlockSpec(memory_space=pl.ANY),
        scratch_shapes=[
            pltpu.VMEM((2, ST, EXT_COLS * LANES), jnp.bfloat16),
            pltpu.VMEM((2, ST, DCOLS * LANES), jnp.float32),
            pltpu.VMEM((KS * ST, 2 * C), jnp.bfloat16),
            pltpu.VMEM((GROUPS, STN, KG, ST, LANES), jnp.bfloat16),
            pltpu.VMEM((GROUPS, STN, KG, ST, LANES), jnp.bfloat16),
            pltpu.VMEM((own, 512, 1024), jnp.bfloat16),
            pltpu.VMEM((CPG, 1024, 2 * LANES), jnp.bfloat16),
            pltpu.VMEM((own, B, KS), jnp.float32),
            pltpu.SemaphoreType.DMA((GROUPS,)),
            pltpu.SemaphoreType.DMA((GROUPS,)),
            pltpu.SemaphoreType.DMA((GROUPS,)),
            pltpu.SemaphoreType.DMA((2,)),
            pltpu.SemaphoreType.DMA,
        ],
        compiler_params=pltpu.CompilerParams(collective_id=0, has_side_effects=True, vmem_limit_bytes=56 << 20),
    )(main, delay, frac, taps, table, offset, index)


def local(samples, filter_taps, frac_delay, station_delay, beam_index):
    main = samples.transpose(1, 0, 2)
    table = jnp.asarray(dft_columns())
    offset = jnp.asarray((column_channels() - C // 2).astype(np.float32) / C)
    return beams(main, station_delay, frac_delay, filter_taps, table, offset, beam_index)


def solution(mesh):
    in_specs = (P("stn", None, "tm"), P(), P("stn"), P("stn"), P())
    out_specs = P("stn", None, "tm")
    return jax.shard_map(local, mesh=mesh, in_specs=in_specs, out_specs=out_specs, check_vma=False)
```

```python
import math

import jax
import jax.numpy as jnp
import ml_dtypes
import numpy as np
from jax import lax
from jax.experimental import pallas as pl
from jax.experimental.pallas import tpu as pltpu
from jax.sharding import PartitionSpec as P

TAPS = 16
C = 384
B = 500
LANES = 128
COLS = C // LANES
DSPEC = 4
STN = 32
ST = 16
KS = 80
KG = KS // 16
GROUPS = 3
CPG = 4
REACH = (TAPS - 1 + DSPEC) * C
SPAN = KS * C
DCOLS = (KS + TAPS - 1) * COLS
PHASES = ((0, 1), (1, 3), (3, 5))
CHUNK = 24
RIM = (TAPS - 1) * COLS + 48 * PHASES[-1][0]
RIM_COLS = SPAN // LANES - RIM
EXT_COLS = DCOLS + 16 - RIM
RELAYS = 3
PIECE = REACH // RELAYS
MESH = pl.DeviceIdType.MESH


def sincos_turns(r):
    h = r * math.pi
    z = h * h
    s = jnp.full_like(r, 1.0 / 6227020800.0)
    for c in (-1.0 / 39916800.0, 1.0 / 362880.0, -1.0 / 5040.0, 1.0 / 120.0, -1.0 / 6.0, 1.0):
        s = s * z + c
    s = s * h
    q = jnp.full_like(r, 1.0 / 479001600.0)
    for c in (-1.0 / 3628800.0, 1.0 / 40320.0, -1.0 / 720.0, 1.0 / 24.0, -0.5, 1.0):
        q = q * z + c
    return 1.0 - 2.0 * s * s, 2.0 * s * q


def column_channels():
    lane = np.arange(LANES)
    dest, sub = lane % STN, lane // STN
    own = C // STN
    return np.stack([dest * own + g * CPG + sub for g in range(GROUPS)])


def dft_columns():
    chan = column_channels()
    n = np.arange(C)
    parts = []
    for g in range(GROUPS):
        angle = 2.0 * np.pi / C * ((n[:, None] * chan[g][None, :]) % C)
        cosine = np.cos(angle) / math.sqrt(C)
        sine = np.sin(angle) / math.sqrt(C)
        upper = np.concatenate([cosine, -sine], axis=1)
        lower = np.concatenate([sine, cosine], axis=1)
        parts.append(np.concatenate([upper, lower], axis=0))
    return np.stack(parts).astype(ml_dtypes.bfloat16)


def butterfly(vregs, lane, widths):
    vregs = list(vregs)
    for j, w in enumerate(widths):
        mask = (lane & w) != 0
        out = list(vregs)
        for i in range(len(vregs)):
            if not i & (1 << j):
                k = i | (1 << j)
                out[i] = jnp.where(mask, pltpu.roll(vregs[k], w, 1), vregs[i])
                out[k] = jnp.where(mask, vregs[k], pltpu.roll(vregs[i], LANES - w, 1))
        vregs = out
    return vregs


def station_rows(values_ref):
    row = lax.broadcasted_iota(jnp.int32, (ST, LANES), 0)
    out = jnp.full((ST, LANES), values_ref[0])
    for i in range(1, ST):
        out = jnp.where(row == i, values_ref[i], out)
    return out


def kernel(main_ref, delay_ref, frac_ref, taps_ref, table_ref, offset_ref, index_ref, out_ref, ext, dly, frames, msg, recv, weights, rhs, relay, send_sem, recv_sem, own_sem, halo_sem, relay_sem, edge_sem):
    me = lax.axis_index("stn")
    tm = lax.axis_index("tm")
    count = lax.axis_size("tm")
    barrier = pltpu.get_barrier_semaphore()

    def greet(i, _):
        pl.semaphore_signal(barrier, inc=1, device_id={"stn": lax.rem(me + i, STN)}, device_id_type=MESH)
        return 0

    lax.fori_loop(1, STN, greet, 0)
    half = count // 2
    edge = half - 1
    far, near = count - RELAYS, half - RELAYS
    plain_from = (tm < count - 1) & (tm != edge)
    plain_to = (tm > 0) & (tm != half)

    def greet_tm(condition, to):
        @pl.when(condition)
        def _():
            pl.semaphore_signal(barrier, inc=1, device_id={"tm": to}, device_id_type=MESH)

    greet_tm(plain_from, tm + 1)
    greet_tm(tm >= far, half)
    greet_tm((tm >= near) & (tm < half), tm + half)
    for i in range(RELAYS - 1):
        greet_tm(tm == edge, near + i)

    delay = station_rows(delay_ref)
    frac = station_rows(frac_ref)
    lane = lax.broadcasted_iota(jnp.int32, (ST, LANES), 1)
    rest = delay & (LANES - 1)
    index = (lane + rest) & (LANES - 1)
    keep = lane < LANES - rest
    bits = [(delay & (LANES << b)) != 0 for b in range(4)]

    ext[:, :, : RIM_COLS * LANES] = main_ref[:, :, RIM * LANES :]
    ext[:, :, RIM_COLS * LANES + REACH :] = jnp.zeros((2, ST, EXT_COLS * LANES - RIM_COLS * LANES - REACH), jnp.bfloat16)

    others = plain_to.astype(jnp.int32) + (tm >= far).astype(jnp.int32)
    others = others + ((tm >= near) & (tm < edge)).astype(jnp.int32) + (tm == half).astype(jnp.int32) * RELAYS
    pl.semaphore_wait(barrier, STN - 1 + others)

    def halo(to):
        return pltpu.make_async_remote_copy(
            src_ref=main_ref.at[:, :, :REACH],
            dst_ref=ext.at[:, :, RIM_COLS * LANES : RIM_COLS * LANES + REACH],
            send_sem=halo_sem.at[0],
            recv_sem=halo_sem.at[1],
            device_id={"tm": to},
            device_id_type=MESH,
        )

    def piece(source, target, to, end, start):
        return pltpu.make_async_remote_copy(
            src_ref=source,
            dst_ref=target,
            send_sem=start,
            recv_sem=end,
            device_id={"tm": to},
            device_id_type=MESH,
        )

    def leave(i):
        return piece(main_ref.at[:, :, i * PIECE : (i + 1) * PIECE], relay, far + i, relay_sem.at[0], edge_sem.at[RELAYS + i])

    def cross():
        return piece(relay, relay, tm - half, relay_sem.at[0], relay_sem.at[1])

    def arrive(i, to):
        at = RIM_COLS * LANES + i * PIECE
        return piece(relay, ext.at[:, :, at : at + PIECE], to, edge_sem.at[i], relay_sem.at[1])

    @pl.when(tm == half)
    def _():
        for i in range(RELAYS):
            leave(i).start()

    @pl.when(plain_to)
    def _():
        halo(tm - 1).start()

    @pl.when(tm == count - 1)
    def _():
        ext[:, :, RIM_COLS * LANES : RIM_COLS * LANES + REACH] = jnp.zeros((2, ST, REACH), jnp.bfloat16)

    def align(source, base, shift):
        for r in range(2):
            cols = []
            for j in range(CHUNK + 16):
                at = pl.multiple_of((base + j - shift) * LANES, LANES)
                cols.append(source[r, :, pl.ds(at, LANES)])
            for b in (3, 2, 1, 0):
                cols = [jnp.where(bits[b], cols[j + (1 << b)], cols[j]) for j in range(len(cols) - (1 << b))]
            turned = [
                jnp.take_along_axis(col.astype(jnp.float32), index, axis=1, mode="promise_in_bounds")
                for col in cols[: CHUNK + 1]
            ]
            for j in range(CHUNK):
                at = pl.multiple_of((base + j) * LANES, LANES)
                dly[r, :, pl.ds(at, LANES)] = jnp.where(keep, turned[j], turned[j + 1])

    per = 8

    def filt(step):
        for r in range(2):
            for m in range(COLS):
                sums = [None] * per
                for j in range(per + TAPS - 1):
                    at = pl.multiple_of((step * per + j) * C + m * LANES, LANES)
                    col = dly[r, :, pl.ds(at, LANES)]
                    for i in range(max(0, j - TAPS + 1), min(per, j + 1)):
                        p = j - i
                        term = col * taps_ref[p : p + 1, m * LANES : (m + 1) * LANES]
                        sums[i] = term if sums[i] is None else sums[i] + term
                for i in range(per):
                    row = pl.multiple_of((step * per + i) * ST, ST)
                    frames[pl.ds(row, ST), r * C + m * LANES : r * C + (m + 1) * LANES] = sums[i].astype(jnp.bfloat16)

    def spectra(g, kg, cosine, sine):
        spec = jnp.dot(frames[kg * 256 : (kg + 1) * 256, :], table_ref[g], preferred_element_type=jnp.float32)
        turned = [[], []]
        for k in range(16):
            re = spec[k * ST : (k + 1) * ST, :LANES]
            im = spec[k * ST : (k + 1) * ST, LANES:]
            turned[0].append((re * cosine - im * sine).astype(jnp.bfloat16))
            turned[1].append((re * sine + im * cosine).astype(jnp.bfloat16))
        blocks = butterfly(turned[0] + turned[1], lane, (1, 2, 4, 8, 16))
        for d in range(STN):
            msg[g, d, kg] = blocks[d]

    def loop(start, stop, step, unroll=1):
        def body(i, _):
            step(i)
            return 0

        lax.fori_loop(start, stop, body, 0, unroll=unroll)

    loop(0, 48 // CHUNK, lambda i: align(main_ref, i * CHUNK, 0))
    for number, (begin, end) in enumerate(PHASES):
        last = number == len(PHASES) - 1
        if last:
            @pl.when(plain_from)
            def _():
                halo(tm).wait_recv()

            @pl.when(tm == edge)
            def _():
                for i in range(RELAYS):
                    arrive(i, tm).wait_recv()

        source, shift = (ext, RIM) if last else (main_ref, 0)
        first_col = (TAPS - 1) * COLS + 48 * begin
        loop(0, (end - begin) * 48 // CHUNK, lambda i: align(source, first_col + i * CHUNK, shift))
        loop(begin * 16 // per, end * 16 // per, filt)
        for g in range(GROUPS):
            cosine, sine = sincos_turns(frac * offset_ref[g : g + 1, :])
            for kg in range(begin, end):
                spectra(g, kg, cosine, sine)

            def post(i, _):
                to = lax.rem(me + i, STN)
                pltpu.make_async_remote_copy(
                    src_ref=msg.at[g, to, begin:end],
                    dst_ref=recv.at[g, me, begin:end],
                    send_sem=send_sem.at[g],
                    recv_sem=recv_sem.at[g],
                    device_id={"stn": to},
                    device_id_type=MESH,
                ).start()
                return 0

            lax.fori_loop(1, STN, post, 0)
            if last:
                pltpu.make_async_copy(msg.at[g, me], recv.at[g, me], own_sem.at[g]).start()

        if number == 0:
            @pl.when((tm >= far) & (tm < count - 1))
            def _():
                cross().wait_recv()
                cross().start()

            @pl.when(tm == count - 1)
            def _():
                cross().wait_recv()
                arrive(RELAYS - 1, edge).start()

        if number == 1:
            for i in range(RELAYS - 1):
                @pl.when(tm == near + i)
                def _():
                    cross().wait_recv()
                    arrive(i, edge).start()

    own = C // STN
    first = (me * own - C // 2).astype(jnp.float32)

    def weigh(at, rows):
        rows = rows.astype(jnp.float32)
        step_re, step_im = sincos_turns(rows * (1.0 / (16 * C)))
        start = rows * first * (1.0 / (16 * C))
        now_re, now_im = sincos_turns(start - jnp.round(start))
        for c in range(own):
            weights[c, pl.ds(at, 16), :512] = now_re.astype(jnp.bfloat16)
            weights[c, pl.ds(at, 16), 512:] = now_im.astype(jnp.bfloat16)
            if c < own - 1:
                now_re, now_im = now_re * step_re - now_im * step_im, now_re * step_im + now_im * step_re

    def weigh_step(i):
        at = pl.multiple_of(i * 16, 16)
        weigh(at, index_ref[pl.ds(at, 16), :])

    loop(0, B // 16, weigh_step)
    tail = B // 16 * 16
    weigh(tail, jnp.concatenate([index_ref[tail:, :], jnp.zeros((16 - B % 16, 512), jnp.int32)], axis=0))

    per_step = 2
    wide = lax.broadcasted_iota(jnp.int32, (per_step * ST, LANES), 1)
    zero = jnp.zeros((per_step * ST, LANES), jnp.bfloat16)
    for g in range(GROUPS):
        pltpu.make_async_copy(msg.at[g, 0 : STN - 1], recv.at[g, 0 : STN - 1], recv_sem.at[g]).wait()
        pltpu.make_async_copy(msg.at[g, me], recv.at[g, me], own_sem.at[g]).wait()

        def unpack(e):
            blocks = [recv[g, pl.ds(e * per_step, per_step), kg].reshape(per_step * ST, LANES) for kg in range(KG)]
            blocks = butterfly(blocks + [zero] * (8 - KG), wide, (16, 32, 64))
            upper = pl.ds(pl.multiple_of(e * per_step * ST, per_step * ST), per_step * ST)
            lower = pl.ds(pl.multiple_of(512 + e * per_step * ST, per_step * ST), per_step * ST)
            for c in range(CPG):
                re, im = blocks[2 * c], blocks[2 * c + 1]
                rhs[c, upper, :LANES] = re
                rhs[c, upper, LANES:] = im
                rhs[c, lower, :LANES] = -im
                rhs[c, lower, LANES:] = re

        loop(0, STN // per_step, unpack, 4)

        def detect(c):
            beam = jnp.dot(weights[g * CPG + c], rhs[c], preferred_element_type=jnp.float32)
            re = beam[:, :LANES]
            im = beam[:, LANES:]
            square = (re * re + im * im) * (1.0 / 512)
            out_ref[g * CPG + c] = square.T[:KS, :B]

        loop(0, CPG, detect)

    for g in range(GROUPS):
        pltpu.make_async_copy(msg.at[g, 0 : STN - 1], recv.at[g, 0 : STN - 1], send_sem.at[g]).wait()

    @pl.when(plain_to)
    def _():
        halo(tm).wait_send()

    @pl.when(tm == half)
    def _():
        for i in range(RELAYS):
            leave(i).wait_send()

    @pl.when((tm >= far) | ((tm >= near) & (tm < edge)))
    def _():
        cross().wait_send()


def beams(main, delay, frac, taps, table, offset, index):
    vmem = pl.BlockSpec(memory_space=pltpu.VMEM)
    smem = pl.BlockSpec(memory_space=pltpu.SMEM)
    own = C // STN
    return pl.pallas_call(
        kernel,
        out_shape=jax.ShapeDtypeStruct((own, KS, B), jnp.float32),
        in_specs=[vmem, smem, smem, vmem, vmem, vmem, vmem],
        out_specs=vmem,
        scratch_shapes=[
            pltpu.VMEM((2, ST, EXT_COLS * LANES), jnp.bfloat16),
            pltpu.VMEM((2, ST, DCOLS * LANES), jnp.float32),
            pltpu.VMEM((KS * ST, 2 * C), jnp.bfloat16),
            pltpu.VMEM((GROUPS, STN, KG, ST, LANES), jnp.bfloat16),
            pltpu.VMEM((GROUPS, STN, KG, ST, LANES), jnp.bfloat16),
            pltpu.VMEM((own, 512, 1024), jnp.bfloat16),
            pltpu.VMEM((CPG, 1024, 2 * LANES), jnp.bfloat16),
            pltpu.VMEM((2, ST, PIECE), jnp.bfloat16),
            pltpu.SemaphoreType.DMA((GROUPS,)),
            pltpu.SemaphoreType.DMA((GROUPS,)),
            pltpu.SemaphoreType.DMA((GROUPS,)),
            pltpu.SemaphoreType.DMA((2,)),
            pltpu.SemaphoreType.DMA((2,)),
            pltpu.SemaphoreType.DMA((2 * RELAYS,)),
        ],
        compiler_params=pltpu.CompilerParams(collective_id=0, has_side_effects=True, vmem_limit_bytes=42 << 20),
    )(main, delay, frac, taps, table, offset, index)


def local(samples, filter_taps, frac_delay, station_delay, beam_index):
    main = samples.transpose(1, 0, 2)
    table = jnp.asarray(dft_columns())
    offset = jnp.asarray((column_channels() - C // 2).astype(np.float32) / C)
    return beams(main, station_delay, frac_delay, filter_taps, table, offset, beam_index).transpose(0, 2, 1)


def solution(mesh):
    in_specs = (P("stn", None, "tm"), P(), P("stn"), P("stn"), P())
    out_specs = P("stn", None, "tm")
    return jax.shard_map(local, mesh=mesh, in_specs=in_specs, out_specs=out_specs, check_vma=False)
```

```python
import math

import jax
import jax.numpy as jnp
import ml_dtypes
import numpy as np
from jax import lax
from jax.experimental import pallas as pl
from jax.experimental.pallas import tpu as pltpu
from jax.sharding import PartitionSpec as P

TAPS = 16
C = 384
B = 500
LANES = 128
COLS = C // LANES
DSPEC = 4
STN = 32
ST = 16
KS = 80
KG = KS // 16
GROUPS = 3
CPG = 4
REACH = (TAPS - 1 + DSPEC) * C
SPAN = KS * C
DCOLS = (KS + TAPS - 1) * COLS
PHASES = ((0, 1), (1, 3), (3, 5))
CHUNK = 24
RIM = (TAPS - 1) * COLS + 48 * PHASES[-1][0]
RIM_COLS = SPAN // LANES - RIM
EXT_COLS = DCOLS + 16 - RIM
RELAYS = 5
CUTS = [REACH // LANES * i // RELAYS * LANES for i in range(RELAYS + 1)]
PIECE = max(b - a for a, b in zip(CUTS, CUTS[1:]))
MESH = pl.DeviceIdType.MESH


def sincos_turns(r):
    h = r * math.pi
    z = h * h
    s = jnp.full_like(r, 1.0 / 6227020800.0)
    for c in (-1.0 / 39916800.0, 1.0 / 362880.0, -1.0 / 5040.0, 1.0 / 120.0, -1.0 / 6.0, 1.0):
        s = s * z + c
    s = s * h
    q = jnp.full_like(r, 1.0 / 479001600.0)
    for c in (-1.0 / 3628800.0, 1.0 / 40320.0, -1.0 / 720.0, 1.0 / 24.0, -0.5, 1.0):
        q = q * z + c
    return 1.0 - 2.0 * s * s, 2.0 * s * q


def column_channels():
    lane = np.arange(LANES)
    dest, sub = lane % STN, lane // STN
    own = C // STN
    return np.stack([dest * own + g * CPG + sub for g in range(GROUPS)])


def dft_columns():
    chan = column_channels()
    n = np.arange(C)
    parts = []
    for g in range(GROUPS):
        angle = 2.0 * np.pi / C * ((n[:, None] * chan[g][None, :]) % C)
        cosine = np.cos(angle) / math.sqrt(C)
        sine = np.sin(angle) / math.sqrt(C)
        upper = np.concatenate([cosine, -sine], axis=1)
        lower = np.concatenate([sine, cosine], axis=1)
        parts.append(np.concatenate([upper, lower], axis=0))
    return np.stack(parts).astype(ml_dtypes.bfloat16)


def butterfly(vregs, lane, widths):
    vregs = list(vregs)
    for j, w in enumerate(widths):
        mask = (lane & w) != 0
        out = list(vregs)
        for i in range(len(vregs)):
            if not i & (1 << j):
                k = i | (1 << j)
                out[i] = jnp.where(mask, pltpu.roll(vregs[k], w, 1), vregs[i])
                out[k] = jnp.where(mask, vregs[k], pltpu.roll(vregs[i], LANES - w, 1))
        vregs = out
    return vregs


def station_rows(values_ref):
    row = lax.broadcasted_iota(jnp.int32, (ST, LANES), 0)
    out = jnp.full((ST, LANES), values_ref[0])
    for i in range(1, ST):
        out = jnp.where(row == i, values_ref[i], out)
    return out


def kernel(main_ref, delay_ref, frac_ref, taps_ref, table_ref, offset_ref, index_ref, out_ref, ext, dly, frames, msg, recv, weights, rhs, relay, send_sem, recv_sem, own_sem, halo_sem, relay_sem, edge_sem, ready_sem):
    me = lax.axis_index("stn")
    tm = lax.axis_index("tm")
    count = lax.axis_size("tm")
    barrier = pltpu.get_barrier_semaphore()

    def greet(i, _):
        pl.semaphore_signal(barrier, inc=1, device_id={"stn": lax.rem(me + i, STN)}, device_id_type=MESH)
        return 0

    lax.fori_loop(1, STN, greet, 0)
    half = count // 2
    edge = half - 1
    far, near = count - RELAYS, half - RELAYS
    plain_from = (tm < count - 1) & (tm != edge)
    plain_to = (tm > 0) & (tm != half)

    def greet_tm(condition, to):
        @pl.when(condition)
        def _():
            pl.semaphore_signal(barrier, inc=1, device_id={"tm": to}, device_id_type=MESH)

    greet_tm(plain_from, tm + 1)
    greet_tm((tm >= near) & (tm < half), tm + half)
    greet_tm((tm >= near) & (tm < edge), edge)
    for i in range(RELAYS):
        greet_tm(tm == half, far + i)

    delay = station_rows(delay_ref)
    frac = station_rows(frac_ref)
    lane = lax.broadcasted_iota(jnp.int32, (ST, LANES), 1)
    rest = delay & (LANES - 1)
    index = (lane + rest) & (LANES - 1)
    keep = lane < LANES - rest
    bits = [(delay & (LANES << b)) != 0 for b in range(4)]

    ext[:, :, : RIM_COLS * LANES] = main_ref[:, :, RIM * LANES :]
    ext[:, :, RIM_COLS * LANES + REACH :] = jnp.zeros((2, ST, EXT_COLS * LANES - RIM_COLS * LANES - REACH), jnp.bfloat16)

    others = plain_to.astype(jnp.int32) + (tm >= far).astype(jnp.int32) * 2 + (tm == edge).astype(jnp.int32) * (RELAYS - 1)
    pl.semaphore_wait(barrier, STN - 1 + others)

    def halo(to):
        return pltpu.make_async_remote_copy(
            src_ref=main_ref.at[:, :, :REACH],
            dst_ref=ext.at[:, :, RIM_COLS * LANES : RIM_COLS * LANES + REACH],
            send_sem=halo_sem.at[0],
            recv_sem=halo_sem.at[1],
            device_id={"tm": to},
            device_id_type=MESH,
        )

    def piece(source, target, to, end, start):
        return pltpu.make_async_remote_copy(
            src_ref=source,
            dst_ref=target,
            send_sem=start,
            recv_sem=end,
            device_id={"tm": to},
            device_id_type=MESH,
        )

    def leave(i):
        width = CUTS[i + 1] - CUTS[i]
        source = main_ref.at[:, :, CUTS[i] : CUTS[i + 1]]
        return piece(source, relay.at[:, :, :width], far + i, relay_sem.at[0], edge_sem.at[RELAYS + i])

    def cross(i):
        part = relay.at[:, :, : CUTS[i + 1] - CUTS[i]]
        return piece(part, part, near + i, relay_sem.at[0], relay_sem.at[1])

    def arrive(i):
        at = RIM_COLS * LANES
        target = ext.at[:, :, at + CUTS[i] : at + CUTS[i + 1]]
        return piece(relay.at[:, :, : CUTS[i + 1] - CUTS[i]], target, edge, edge_sem.at[i], relay_sem.at[1])

    def ready(condition, to):
        @pl.when(condition)
        def _():
            pl.semaphore_signal(ready_sem, inc=1, device_id={"tm": to}, device_id_type=MESH)

    ready(tm >= far, half)
    for i in range(RELAYS - 1):
        ready(tm == edge, near + i)

    @pl.when(plain_to)
    def _():
        halo(tm - 1).start()

    @pl.when(tm == count - 1)
    def _():
        ext[:, :, RIM_COLS * LANES : RIM_COLS * LANES + REACH] = jnp.zeros((2, ST, REACH), jnp.bfloat16)

    def align(source, base, shift):
        for r in range(2):
            cols = []
            for j in range(CHUNK + 16):
                at = pl.multiple_of((base + j - shift) * LANES, LANES)
                cols.append(source[r, :, pl.ds(at, LANES)])
            for b in (3, 2, 1, 0):
                cols = [jnp.where(bits[b], cols[j + (1 << b)], cols[j]) for j in range(len(cols) - (1 << b))]
            turned = [
                jnp.take_along_axis(col.astype(jnp.float32), index, axis=1, mode="promise_in_bounds")
                for col in cols[: CHUNK + 1]
            ]
            for j in range(CHUNK):
                at = pl.multiple_of((base + j) * LANES, LANES)
                dly[r, :, pl.ds(at, LANES)] = jnp.where(keep, turned[j], turned[j + 1])

    per = 8

    def filt(step):
        for r in range(2):
            for m in range(COLS):
                sums = [None] * per
                for j in range(per + TAPS - 1):
                    at = pl.multiple_of((step * per + j) * C + m * LANES, LANES)
                    col = dly[r, :, pl.ds(at, LANES)]
                    for i in range(max(0, j - TAPS + 1), min(per, j + 1)):
                        p = j - i
                        term = col * taps_ref[p : p + 1, m * LANES : (m + 1) * LANES]
                        sums[i] = term if sums[i] is None else sums[i] + term
                for i in range(per):
                    row = pl.multiple_of((step * per + i) * ST, ST)
                    frames[pl.ds(row, ST), r * C + m * LANES : r * C + (m + 1) * LANES] = sums[i].astype(jnp.bfloat16)

    def spectra(g, kg, cosine, sine):
        spec = jnp.dot(frames[kg * 256 : (kg + 1) * 256, :], table_ref[g], preferred_element_type=jnp.float32)
        turned = [[], []]
        for k in range(16):
            re = spec[k * ST : (k + 1) * ST, :LANES]
            im = spec[k * ST : (k + 1) * ST, LANES:]
            turned[0].append((re * cosine - im * sine).astype(jnp.bfloat16))
            turned[1].append((re * sine + im * cosine).astype(jnp.bfloat16))
        blocks = butterfly(turned[0] + turned[1], lane, (1, 2, 4, 8, 16))
        for d in range(STN):
            msg[g, d, kg] = blocks[d]

    def loop(start, stop, step, unroll=1):
        def body(i, _):
            step(i)
            return 0

        lax.fori_loop(start, stop, body, 0, unroll=unroll)

    loop(0, 48 // CHUNK, lambda i: align(main_ref, i * CHUNK, 0))
    for number, (begin, end) in enumerate(PHASES):
        last = number == len(PHASES) - 1
        if last:
            @pl.when(plain_from)
            def _():
                halo(tm).wait_recv()

            @pl.when(tm == edge)
            def _():
                for i in range(RELAYS):
                    arrive(i).wait_recv()

        source, shift = (ext, RIM) if last else (main_ref, 0)
        first_col = (TAPS - 1) * COLS + 48 * begin
        loop(0, (end - begin) * 48 // CHUNK, lambda i: align(source, first_col + i * CHUNK, shift))
        loop(begin * 16 // per, end * 16 // per, filt)
        for g in range(GROUPS):
            cosine, sine = sincos_turns(frac * offset_ref[g : g + 1, :])
            for kg in range(begin, end):
                spectra(g, kg, cosine, sine)

            def post(i, _):
                to = lax.rem(me + i, STN)
                pltpu.make_async_remote_copy(
                    src_ref=msg.at[g, to, begin:end],
                    dst_ref=recv.at[g, me, begin:end],
                    send_sem=send_sem.at[g],
                    recv_sem=recv_sem.at[g],
                    device_id={"stn": to},
                    device_id_type=MESH,
                ).start()
                return 0

            lax.fori_loop(1, STN, post, 0)
            if last:
                pltpu.make_async_copy(msg.at[g, me], recv.at[g, me], own_sem.at[g]).start()

        if number == 0:
            @pl.when(tm == half)
            def _():
                pl.semaphore_wait(ready_sem, RELAYS)
                for i in range(RELAYS):
                    leave(i).start()

            for i in range(RELAYS):
                @pl.when(tm == far + i)
                def _():
                    cross(i).wait_recv()
                    (cross(i) if i < RELAYS - 1 else arrive(i)).start()

        if number == 1:
            for i in range(RELAYS - 1):
                @pl.when(tm == near + i)
                def _():
                    pl.semaphore_wait(ready_sem, 1)
                    cross(i).wait_recv()
                    arrive(i).start()

    own = C // STN
    first = (me * own - C // 2).astype(jnp.float32)

    def weigh(at, rows):
        rows = rows.astype(jnp.float32)
        step_re, step_im = sincos_turns(rows * (1.0 / (16 * C)))
        start = rows * first * (1.0 / (16 * C))
        now_re, now_im = sincos_turns(start - jnp.round(start))
        for c in range(own):
            weights[c, pl.ds(at, 16), :512] = now_re.astype(jnp.bfloat16)
            weights[c, pl.ds(at, 16), 512:] = now_im.astype(jnp.bfloat16)
            if c < own - 1:
                now_re, now_im = now_re * step_re - now_im * step_im, now_re * step_im + now_im * step_re

    def weigh_step(i):
        at = pl.multiple_of(i * 16, 16)
        weigh(at, index_ref[pl.ds(at, 16), :])

    loop(0, B // 16, weigh_step)
    tail = B // 16 * 16
    weigh(tail, jnp.concatenate([index_ref[tail:, :], jnp.zeros((16 - B % 16, 512), jnp.int32)], axis=0))

    per_step = 2
    wide = lax.broadcasted_iota(jnp.int32, (per_step * ST, LANES), 1)
    zero = jnp.zeros((per_step * ST, LANES), jnp.bfloat16)
    for g in range(GROUPS):
        pltpu.make_async_copy(msg.at[g, 0 : STN - 1], recv.at[g, 0 : STN - 1], recv_sem.at[g]).wait()
        pltpu.make_async_copy(msg.at[g, me], recv.at[g, me], own_sem.at[g]).wait()

        def unpack(e):
            blocks = [recv[g, pl.ds(e * per_step, per_step), kg].reshape(per_step * ST, LANES) for kg in range(KG)]
            blocks = butterfly(blocks + [zero] * (8 - KG), wide, (16, 32, 64))
            upper = pl.ds(pl.multiple_of(e * per_step * ST, per_step * ST), per_step * ST)
            lower = pl.ds(pl.multiple_of(512 + e * per_step * ST, per_step * ST), per_step * ST)
            for c in range(CPG):
                re, im = blocks[2 * c], blocks[2 * c + 1]
                rhs[c, upper, :LANES] = re
                rhs[c, upper, LANES:] = im
                rhs[c, lower, :LANES] = -im
                rhs[c, lower, LANES:] = re

        loop(0, STN // per_step, unpack, 4)

        def detect(c):
            beam = jnp.dot(weights[g * CPG + c], rhs[c], preferred_element_type=jnp.float32)
            re = beam[:, :LANES]
            im = beam[:, LANES:]
            square = (re * re + im * im) * (1.0 / 512)
            out_ref[g * CPG + c] = square.T[:KS, :B]

        loop(0, CPG, detect)

    for g in range(GROUPS):
        pltpu.make_async_copy(msg.at[g, 0 : STN - 1], recv.at[g, 0 : STN - 1], send_sem.at[g]).wait()

    @pl.when(plain_to)
    def _():
        halo(tm).wait_send()

    @pl.when(tm == half)
    def _():
        for i in range(RELAYS):
            leave(i).wait_send()

    for i in range(RELAYS):
        @pl.when((tm == far + i) | (tm == near + i) & (tm < edge))
        def _():
            cross(i).wait_send()


def beams(main, delay, frac, taps, table, offset, index):
    vmem = pl.BlockSpec(memory_space=pltpu.VMEM)
    smem = pl.BlockSpec(memory_space=pltpu.SMEM)
    own = C // STN
    return pl.pallas_call(
        kernel,
        out_shape=jax.ShapeDtypeStruct((own, KS, B), jnp.float32),
        in_specs=[vmem, smem, smem, vmem, vmem, vmem, vmem],
        out_specs=vmem,
        scratch_shapes=[
            pltpu.VMEM((2, ST, EXT_COLS * LANES), jnp.bfloat16),
            pltpu.VMEM((2, ST, DCOLS * LANES), jnp.float32),
            pltpu.VMEM((KS * ST, 2 * C), jnp.bfloat16),
            pltpu.VMEM((GROUPS, STN, KG, ST, LANES), jnp.bfloat16),
            pltpu.VMEM((GROUPS, STN, KG, ST, LANES), jnp.bfloat16),
            pltpu.VMEM((own, 512, 1024), jnp.bfloat16),
            pltpu.VMEM((CPG, 1024, 2 * LANES), jnp.bfloat16),
            pltpu.VMEM((2, ST, PIECE), jnp.bfloat16),
            pltpu.SemaphoreType.DMA((GROUPS,)),
            pltpu.SemaphoreType.DMA((GROUPS,)),
            pltpu.SemaphoreType.DMA((GROUPS,)),
            pltpu.SemaphoreType.DMA((2,)),
            pltpu.SemaphoreType.DMA((2,)),
            pltpu.SemaphoreType.DMA((2 * RELAYS,)),
            pltpu.SemaphoreType.REGULAR,
        ],
        compiler_params=pltpu.CompilerParams(collective_id=0, has_side_effects=True, vmem_limit_bytes=42 << 20),
    )(main, delay, frac, taps, table, offset, index)


def local(samples, filter_taps, frac_delay, station_delay, beam_index):
    main = samples.transpose(1, 0, 2)
    table = jnp.asarray(dft_columns())
    offset = jnp.asarray((column_channels() - C // 2).astype(np.float32) / C)
    return beams(main, station_delay, frac_delay, filter_taps, table, offset, beam_index).transpose(0, 2, 1)


def solution(mesh):
    in_specs = (P("stn", None, "tm"), P(), P("stn"), P("stn"), P())
    out_specs = P("stn", None, "tm")
    return jax.shard_map(local, mesh=mesh, in_specs=in_specs, out_specs=out_specs, check_vma=False)
```

```python
import math

import jax
import jax.numpy as jnp
import ml_dtypes
import numpy as np
from jax import lax
from jax.experimental import pallas as pl
from jax.experimental.pallas import tpu as pltpu
from jax.sharding import PartitionSpec as P

TAPS = 16
C = 384
B = 500
LANES = 128
COLS = C // LANES
DSPEC = 4
STN = 32
ST = 16
KS = 80
KG = KS // 16
GROUPS = 3
CPG = 4
REACH = (TAPS - 1 + DSPEC) * C
SPAN = KS * C
DCOLS = (KS + TAPS - 1) * COLS
PHASES = ((0, 1), (1, 3), (3, 5))
CHUNK = 24
RIM = (TAPS - 1) * COLS + 48 * PHASES[-1][0]
RIM_COLS = SPAN // LANES - RIM
EXT_COLS = DCOLS + 16 - RIM
RELAYS = 5
CUTS = [REACH // LANES * i // RELAYS * LANES for i in range(RELAYS + 1)]
PIECE = max(b - a for a, b in zip(CUTS, CUTS[1:]))
MESH = pl.DeviceIdType.MESH


def sincos_turns(r):
    h = r * math.pi
    z = h * h
    s = jnp.full_like(r, 1.0 / 6227020800.0)
    for c in (-1.0 / 39916800.0, 1.0 / 362880.0, -1.0 / 5040.0, 1.0 / 120.0, -1.0 / 6.0, 1.0):
        s = s * z + c
    s = s * h
    q = jnp.full_like(r, 1.0 / 479001600.0)
    for c in (-1.0 / 3628800.0, 1.0 / 40320.0, -1.0 / 720.0, 1.0 / 24.0, -0.5, 1.0):
        q = q * z + c
    return 1.0 - 2.0 * s * s, 2.0 * s * q


def column_channels():
    lane = np.arange(LANES)
    dest, sub = lane % STN, lane // STN
    own = C // STN
    return np.stack([dest * own + g * CPG + sub for g in range(GROUPS)])


def dft_columns():
    chan = column_channels()
    n = np.arange(C)
    parts = []
    for g in range(GROUPS):
        angle = 2.0 * np.pi / C * ((n[:, None] * chan[g][None, :]) % C)
        cosine = np.cos(angle) / math.sqrt(C)
        sine = np.sin(angle) / math.sqrt(C)
        upper = np.concatenate([cosine, -sine], axis=1)
        lower = np.concatenate([sine, cosine], axis=1)
        parts.append(np.concatenate([upper, lower], axis=0))
    return np.stack(parts).astype(ml_dtypes.bfloat16)


def butterfly(vregs, lane, widths):
    vregs = list(vregs)
    for j, w in enumerate(widths):
        mask = (lane & w) != 0
        out = list(vregs)
        for i in range(len(vregs)):
            if not i & (1 << j):
                k = i | (1 << j)
                out[i] = jnp.where(mask, pltpu.roll(vregs[k], w, 1), vregs[i])
                out[k] = jnp.where(mask, vregs[k], pltpu.roll(vregs[i], LANES - w, 1))
        vregs = out
    return vregs


def station_rows(values_ref):
    row = lax.broadcasted_iota(jnp.int32, (ST, LANES), 0)
    out = jnp.full((ST, LANES), values_ref[0])
    for i in range(1, ST):
        out = jnp.where(row == i, values_ref[i], out)
    return out


def kernel(main_ref, delay_ref, frac_ref, taps_ref, table_ref, offset_ref, index_ref, out_ref, ext, dly, frames, msg, recv, weights, rhs, relay, send_sem, recv_sem, own_sem, halo_sem, relay_sem, edge_sem, ready_sem):
    me = lax.axis_index("stn")
    tm = lax.axis_index("tm")
    count = lax.axis_size("tm")
    barrier = pltpu.get_barrier_semaphore()

    def greet(i, _):
        pl.semaphore_signal(barrier, inc=1, device_id={"stn": lax.rem(me + i, STN)}, device_id_type=MESH)
        return 0

    lax.fori_loop(1, STN, greet, 0)
    half = count // 2
    edge = half - 1
    far, near = count - RELAYS, half - RELAYS
    plain_from = (tm < count - 1) & (tm != edge)
    plain_to = (tm > 0) & (tm != half)

    def greet_tm(condition, to):
        @pl.when(condition)
        def _():
            pl.semaphore_signal(barrier, inc=1, device_id={"tm": to}, device_id_type=MESH)

    greet_tm(plain_from, tm + 1)
    greet_tm((tm >= near) & (tm < half), tm + half)
    greet_tm((tm >= near) & (tm < edge), edge)
    for i in range(RELAYS):
        greet_tm(tm == half, far + i)

    delay = station_rows(delay_ref)
    frac = station_rows(frac_ref)
    lane = lax.broadcasted_iota(jnp.int32, (ST, LANES), 1)
    rest = delay & (LANES - 1)
    index = (lane + rest) & (LANES - 1)
    keep = lane < LANES - rest
    bits = [(delay & (LANES << b)) != 0 for b in range(4)]

    ext[:, :, : RIM_COLS * LANES] = main_ref[:, :, RIM * LANES :]
    ext[:, :, RIM_COLS * LANES + REACH :] = jnp.zeros((2, ST, EXT_COLS * LANES - RIM_COLS * LANES - REACH), jnp.bfloat16)

    others = plain_to.astype(jnp.int32) + (tm >= far).astype(jnp.int32) * 2 + (tm == edge).astype(jnp.int32) * (RELAYS - 1)
    pl.semaphore_wait(barrier, STN - 1 + others)

    def halo(to):
        return pltpu.make_async_remote_copy(
            src_ref=main_ref.at[:, :, :REACH],
            dst_ref=ext.at[:, :, RIM_COLS * LANES : RIM_COLS * LANES + REACH],
            send_sem=halo_sem.at[0],
            recv_sem=halo_sem.at[1],
            device_id={"tm": to},
            device_id_type=MESH,
        )

    def piece(source, target, to, end, start):
        return pltpu.make_async_remote_copy(
            src_ref=source,
            dst_ref=target,
            send_sem=start,
            recv_sem=end,
            device_id={"tm": to},
            device_id_type=MESH,
        )

    def leave(i):
        width = CUTS[i + 1] - CUTS[i]
        source = main_ref.at[:, :, CUTS[i] : CUTS[i + 1]]
        return piece(source, relay.at[:, :, :width], far + i, relay_sem.at[0], edge_sem.at[RELAYS + i])

    def cross(i):
        part = relay.at[:, :, : CUTS[i + 1] - CUTS[i]]
        return piece(part, part, near + i, relay_sem.at[0], relay_sem.at[1])

    def arrive(i):
        at = RIM_COLS * LANES
        target = ext.at[:, :, at + CUTS[i] : at + CUTS[i + 1]]
        return piece(relay.at[:, :, : CUTS[i + 1] - CUTS[i]], target, edge, edge_sem.at[i], relay_sem.at[1])

    def ready(condition, to):
        @pl.when(condition)
        def _():
            pl.semaphore_signal(ready_sem, inc=1, device_id={"tm": to}, device_id_type=MESH)

    ready(tm >= far, half)
    for i in range(RELAYS - 1):
        ready(tm == edge, near + i)

    @pl.when(plain_to)
    def _():
        halo(tm - 1).start()

    @pl.when(tm == count - 1)
    def _():
        ext[:, :, RIM_COLS * LANES : RIM_COLS * LANES + REACH] = jnp.zeros((2, ST, REACH), jnp.bfloat16)

    def align(source, base, shift):
        for r in range(2):
            cols = []
            for j in range(CHUNK + 16):
                at = pl.multiple_of((base + j - shift) * LANES, LANES)
                cols.append(source[r, :, pl.ds(at, LANES)])
            for b in (3, 2, 1, 0):
                cols = [jnp.where(bits[b], cols[j + (1 << b)], cols[j]) for j in range(len(cols) - (1 << b))]
            turned = [
                jnp.take_along_axis(col.astype(jnp.float32), index, axis=1, mode="promise_in_bounds")
                for col in cols[: CHUNK + 1]
            ]
            for j in range(CHUNK):
                at = pl.multiple_of((base + j) * LANES, LANES)
                dly[r, :, pl.ds(at, LANES)] = jnp.where(keep, turned[j], turned[j + 1])

    per = 8

    def filt(step):
        for r in range(2):
            for m in range(COLS):
                sums = [None] * per
                for j in range(per + TAPS - 1):
                    at = pl.multiple_of((step * per + j) * C + m * LANES, LANES)
                    col = dly[r, :, pl.ds(at, LANES)]
                    for i in range(max(0, j - TAPS + 1), min(per, j + 1)):
                        p = j - i
                        term = col * taps_ref[p : p + 1, m * LANES : (m + 1) * LANES]
                        sums[i] = term if sums[i] is None else sums[i] + term
                for i in range(per):
                    row = pl.multiple_of((step * per + i) * ST, ST)
                    frames[pl.ds(row, ST), r * C + m * LANES : r * C + (m + 1) * LANES] = sums[i].astype(jnp.bfloat16)

    def spectra(g, kg, cosine, sine):
        spec = jnp.dot(frames[kg * 256 : (kg + 1) * 256, :], table_ref[g], preferred_element_type=jnp.float32)
        turned = [[], []]
        for k in range(16):
            re = spec[k * ST : (k + 1) * ST, :LANES]
            im = spec[k * ST : (k + 1) * ST, LANES:]
            turned[0].append((re * cosine - im * sine).astype(jnp.bfloat16))
            turned[1].append((re * sine + im * cosine).astype(jnp.bfloat16))
        blocks = butterfly(turned[0] + turned[1], lane, (1, 2, 4, 8, 16))
        for d in range(STN):
            msg[g, d, kg] = blocks[d]

    def loop(start, stop, step, unroll=1):
        def body(i, _):
            step(i)
            return 0

        lax.fori_loop(start, stop, body, 0, unroll=unroll)

    loop(0, 48 // CHUNK, lambda i: align(main_ref, i * CHUNK, 0))
    for number, (begin, end) in enumerate(PHASES):
        last = number == len(PHASES) - 1
        if last:
            @pl.when(plain_from)
            def _():
                halo(tm).wait_recv()

            @pl.when(tm == edge)
            def _():
                for i in range(RELAYS):
                    arrive(i).wait_recv()

        source, shift = (ext, RIM) if last else (main_ref, 0)
        first_col = (TAPS - 1) * COLS + 48 * begin
        loop(0, (end - begin) * 48 // CHUNK, lambda i: align(source, first_col + i * CHUNK, shift))
        loop(begin * 16 // per, end * 16 // per, filt)
        for g in range(GROUPS):
            cosine, sine = sincos_turns(frac * offset_ref[g : g + 1, :])
            for kg in range(begin, end):
                spectra(g, kg, cosine, sine)

            def post(i, _):
                to = lax.rem(me + i, STN)
                pltpu.make_async_remote_copy(
                    src_ref=msg.at[g, to, begin:end],
                    dst_ref=recv.at[g, me, begin:end],
                    send_sem=send_sem.at[g],
                    recv_sem=recv_sem.at[g],
                    device_id={"stn": to},
                    device_id_type=MESH,
                ).start()
                return 0

            lax.fori_loop(1, STN, post, 0)
            if last:
                pltpu.make_async_copy(msg.at[g, me], recv.at[g, me], own_sem.at[g]).start()

        if number == 0:
            @pl.when(tm == half)
            def _():
                pl.semaphore_wait(ready_sem, RELAYS)
                for i in range(RELAYS):
                    leave(i).start()

            for i in range(RELAYS):
                @pl.when(tm == far + i)
                def _():
                    cross(i).wait_recv()
                    (cross(i) if i < RELAYS - 1 else arrive(i)).start()

        if number == 1:
            for i in range(RELAYS - 1):
                @pl.when(tm == near + i)
                def _():
                    pl.semaphore_wait(ready_sem, 1)
                    cross(i).wait_recv()
                    arrive(i).start()

    own = C // STN
    first = (me * own - C // 2).astype(jnp.float32)

    def weigh(at, rows):
        rows = rows.astype(jnp.float32)
        step_re, step_im = sincos_turns(rows * (1.0 / (16 * C)))
        start = rows * first * (1.0 / (16 * C))
        now_re, now_im = sincos_turns(start - jnp.round(start))
        for c in range(own):
            weights[c, pl.ds(at, 16), :512] = now_re.astype(jnp.bfloat16)
            weights[c, pl.ds(at, 16), 512:] = now_im.astype(jnp.bfloat16)
            if c < own - 1:
                now_re, now_im = now_re * step_re - now_im * step_im, now_re * step_im + now_im * step_re

    def weigh_step(i):
        at = pl.multiple_of(i * 16, 16)
        weigh(at, index_ref[pl.ds(at, 16), :])

    loop(0, B // 16, weigh_step)
    tail = B // 16 * 16
    weigh(tail, jnp.concatenate([index_ref[tail:, :], jnp.zeros((16 - B % 16, 512), jnp.int32)], axis=0))

    per_step = 2
    wide = lax.broadcasted_iota(jnp.int32, (per_step * ST, LANES), 1)
    zero = jnp.zeros((per_step * ST, LANES), jnp.bfloat16)
    for g in range(GROUPS):
        pltpu.make_async_copy(msg.at[g, 0 : STN - 1], recv.at[g, 0 : STN - 1], recv_sem.at[g]).wait()
        pltpu.make_async_copy(msg.at[g, me], recv.at[g, me], own_sem.at[g]).wait()

        def unpack(e):
            blocks = [recv[g, pl.ds(e * per_step, per_step), kg].reshape(per_step * ST, LANES) for kg in range(KG)]
            blocks = butterfly(blocks + [zero] * (8 - KG), wide, (16, 32, 64))
            upper = pl.ds(pl.multiple_of(e * per_step * ST, per_step * ST), per_step * ST)
            lower = pl.ds(pl.multiple_of(512 + e * per_step * ST, per_step * ST), per_step * ST)
            for c in range(CPG):
                re, im = blocks[2 * c], blocks[2 * c + 1]
                rhs[c, upper, :LANES] = re
                rhs[c, upper, LANES:] = im
                rhs[c, lower, :LANES] = -im
                rhs[c, lower, LANES:] = re

        loop(0, STN // per_step, unpack, 4)

        def detect(c):
            beam = jnp.dot(weights[g * CPG + c], rhs[c], preferred_element_type=jnp.float32)
            re = beam[:, :LANES]
            im = beam[:, LANES:]
            square = (re * re + im * im) * (1.0 / 512)
            out_ref[g * CPG + c] = square.T[:KS, :B]

        loop(0, CPG, detect, CPG)

    for g in range(GROUPS):
        pltpu.make_async_copy(msg.at[g, 0 : STN - 1], recv.at[g, 0 : STN - 1], send_sem.at[g]).wait()

    @pl.when(plain_to)
    def _():
        halo(tm).wait_send()

    @pl.when(tm == half)
    def _():
        for i in range(RELAYS):
            leave(i).wait_send()

    for i in range(RELAYS):
        @pl.when((tm == far + i) | (tm == near + i) & (tm < edge))
        def _():
            cross(i).wait_send()


def beams(main, delay, frac, taps, table, offset, index):
    vmem = pl.BlockSpec(memory_space=pltpu.VMEM)
    smem = pl.BlockSpec(memory_space=pltpu.SMEM)
    own = C // STN
    return pl.pallas_call(
        kernel,
        out_shape=jax.ShapeDtypeStruct((own, KS, B), jnp.float32),
        in_specs=[vmem, smem, smem, vmem, vmem, vmem, vmem],
        out_specs=vmem,
        scratch_shapes=[
            pltpu.VMEM((2, ST, EXT_COLS * LANES), jnp.bfloat16),
            pltpu.VMEM((2, ST, DCOLS * LANES), jnp.float32),
            pltpu.VMEM((KS * ST, 2 * C), jnp.bfloat16),
            pltpu.VMEM((GROUPS, STN, KG, ST, LANES), jnp.bfloat16),
            pltpu.VMEM((GROUPS, STN, KG, ST, LANES), jnp.bfloat16),
            pltpu.VMEM((own, 512, 1024), jnp.bfloat16),
            pltpu.VMEM((CPG, 1024, 2 * LANES), jnp.bfloat16),
            pltpu.VMEM((2, ST, PIECE), jnp.bfloat16),
            pltpu.SemaphoreType.DMA((GROUPS,)),
            pltpu.SemaphoreType.DMA((GROUPS,)),
            pltpu.SemaphoreType.DMA((GROUPS,)),
            pltpu.SemaphoreType.DMA((2,)),
            pltpu.SemaphoreType.DMA((2,)),
            pltpu.SemaphoreType.DMA((2 * RELAYS,)),
            pltpu.SemaphoreType.REGULAR,
        ],
        compiler_params=pltpu.CompilerParams(collective_id=0, has_side_effects=True, vmem_limit_bytes=42 << 20),
    )(main, delay, frac, taps, table, offset, index)


def local(samples, filter_taps, frac_delay, station_delay, beam_index):
    main = samples.transpose(1, 0, 2)
    table = jnp.asarray(dft_columns())
    offset = jnp.asarray((column_channels() - C // 2).astype(np.float32) / C)
    return beams(main, station_delay, frac_delay, filter_taps, table, offset, beam_index).transpose(0, 2, 1)


def solution(mesh):
    in_specs = (P("stn", None, "tm"), P(), P("stn"), P("stn"), P())
    out_specs = P("stn", None, "tm")
    return jax.shard_map(local, mesh=mesh, in_specs=in_specs, out_specs=out_specs, check_vma=False)
```
